512 devices in a mesh: inp: 8 (over x, core), out: 8 (over z_hi, y), dep: 8 (over z_lo).
Axes of the slice: x: 4, y: 4, z: 16 (z_hi: 2, z_lo: 8; z = z_hi * 8 + z_lo), core: 2. Of those that a mesh axis runs over, the one named last changes fastest.
Arguments:
- inputs: bfloat16 [1024, 4096], P('dep', 'inp'), may hold values from -6 to 6
- out_grad: bfloat16 [1024, 4096], P('dep', 'inp'), may hold values from -6 to 6
- gate_weight: bfloat16 [14336, 4096], P(('out', 'dep'), 'inp'), may hold values from -0.09375 to 0.09375
- up_weight: bfloat16 [14336, 4096], P(('out', 'dep'), 'inp'), may hold values from -0.09375 to 0.09375
- down_weight: bfloat16 [14336, 4096], P(('out', 'dep'), 'inp'), may hold values from -0.046875 to 0.046875
Outputs:
- input_grad: bfloat16 [1024, 4096], P(('dep', 'out'), 'inp')
- gate_grad: bfloat16 [14336, 4096], P(('out', 'dep'), 'inp')
- up_grad: bfloat16 [14336, 4096], P(('out', 'dep'), 'inp')
- down_grad: bfloat16 [14336, 4096], P(('out', 'dep'), 'inp')
The draws below stay inside these ranges and needn't reach their ends.
All inputs are finite; a program needn't handle non-finite values.
Results may differ from the reference program's by a relative error of at most 0.005.
Values may be sent and summed in bfloat16 or wider, within the bound.
A program may use at most 64 MiB of HBM per device.

```python
import jax
import jax.numpy as jnp

D = 4096
FF = 14336
TOKENS = 1024


def block_levels(own_key, extent, shards, least, largest):
    def one(axis_at, parts):
        heights = jax.random.uniform(jax.random.fold_in(jax.random.fold_in(own_key, 6), axis_at), (parts,), jnp.float32, least / len(shards), largest / len(shards))
        return jnp.repeat(jnp.exp(heights), extent[axis_at] // parts).reshape((-1,) + (1,) * (len(extent) - axis_at - 1))

    gain = one(*shards[0])
    for cut in shards[1:]:
        gain = gain * one(*cut)
    return gain


def bell_draw(stream_key, extent, spread, most, pieces=(), dtype=jnp.bfloat16):
    level = block_levels(stream_key, extent, pieces, -0.22, 0.18) if pieces else 1.0
    entries = jax.random.normal(stream_key, extent, jnp.float32) * spread * level
    return jnp.minimum(jnp.maximum(entries, -most), most).astype(dtype)


def setup_inputs(seed: int = 0) -> dict:
    arg_keys = jax.random.split(jax.random.key(seed), 6)
    return {
        "inputs": bell_draw(arg_keys[0], (TOKENS, D), 1.0, 6.0, ((0, 8), (1, 8))),
        "out_grad": bell_draw(arg_keys[1], (TOKENS, D), 0.5, 6.0, ((0, 8), (1, 8))),
        "gate_weight": bell_draw(arg_keys[2], (FF, D), D ** -0.5, 0.09375, ((0, 64), (1, 8))),
        "up_weight": bell_draw(arg_keys[3], (FF, D), D ** -0.5, 0.09375, ((0, 64), (1, 8))),
        "down_weight": bell_draw(arg_keys[4], (FF, D), FF ** -0.5, 0.046875, ((0, 64), (1, 8))),
    }


def reference(inputs, out_grad, gate_weight, up_weight, down_weight):
    gate = jnp.dot(inputs, gate_weight.T, preferred_element_type=jnp.float32)
    up = jnp.dot(inputs, up_weight.T, preferred_element_type=jnp.float32)
    sig = jax.nn.sigmoid(gate)
    hidden = (gate * sig * up).astype(jnp.bfloat16)
    hidden_grad = jnp.dot(out_grad, down_weight.T, preferred_element_type=jnp.float32)
    gate_delta = (hidden_grad * up * sig * (1.0 + gate * (1.0 - sig))).astype(jnp.bfloat16)
    up_delta = (hidden_grad * gate * sig).astype(jnp.bfloat16)
    gate_grad = jnp.dot(gate_delta.T, inputs, preferred_element_type=jnp.float32).astype(jnp.bfloat16)
    up_grad = jnp.dot(up_delta.T, inputs, preferred_element_type=jnp.float32).astype(jnp.bfloat16)
    down_grad = jnp.dot(hidden.T, out_grad, preferred_element_type=jnp.float32).astype(jnp.bfloat16)
    input_grad = jnp.dot(gate_delta, gate_weight, preferred_element_type=jnp.float32)
    input_grad = input_grad + jnp.dot(up_delta, up_weight, preferred_element_type=jnp.float32)
    return input_grad.astype(jnp.bfloat16), gate_grad, up_grad, down_grad
```

```python
import functools

import jax
import jax.numpy as jnp
from jax import lax
from jax.experimental import pallas as pl
from jax.experimental.pallas import tpu as pltpu
from jax.sharding import PartitionSpec as P

MESH = pl.DeviceIdType.MESH
BF16, F32 = jnp.bfloat16, jnp.float32
T, R, H, HP, K = 128, 512, 224, 256, 16
CHUNKS = ((0,), (-1, 1), (-2, 2), (-3, 3), (4,))
N_SEM = 160


def kernel(
    x_hbm, g_hbm, wg_hbm, wu_hbm, wd_hbm, ig_out, gg_out, ug_out, dg_out,
    xg, gg, wgu, wd, acc, zr, zf, local_sem, send_sem, recv_sem, *bufs,
):
    inp, out, zl = lax.axis_index("inp"), lax.axis_index("out"), lax.axis_index("dep")
    x, c, y, zh = inp // 2, inp % 2, out % 4, out // 4
    z = zh * 8 + zl

    def at(dx=0, dc=0, dy=0, dz=0):
        zz = (z + dz) % 16
        return {
            "inp": ((x + dx) % 4) * 2 + (c + dc) % 2,
            "out": (zz // 8) * 4 + (y + dy) % 4,
            "dep": zz % 8,
        }

    partners = [dict(dc=1)] + [dict(dx=d) for d in (1, 2, 3)]
    partners += [dict(dy=d) for d in (1, 2, 3)] + [dict(dz=d) for d in range(1, 16)]

    pf, pb, cr, sf, xs, xr, hg, igf, igb, yr, zs = (
        bufs[i * len(CHUNKS) : (i + 1) * len(CHUNKS)] for i in range(11)
    )
    count = iter(range(N_SEM))
    sent = []

    def send(src, dst, where):
        i = next(count)
        copy = pltpu.make_async_remote_copy(
            src_ref=src, dst_ref=dst, send_sem=send_sem.at[i], recv_sem=recv_sem.at[i],
            device_id=at(**where), device_id_type=MESH,
        )
        copy.start()
        sent.append(copy)
        return copy

    local = []

    def fetch(src, dst):
        copy = pltpu.make_async_copy(src, dst, local_sem.at[len(local)])
        copy.start()
        local.append(copy)

    fetch(x_hbm, xg.at[zl])
    fetch(wg_hbm, wgu.at[pl.ds(0, H)])
    fetch(wu_hbm, wgu.at[pl.ds(HP, H)])
    fetch(wd_hbm, wd.at[pl.ds(0, H)])
    fetch(g_hbm, gg.at[zl])

    barrier = pltpu.get_barrier_semaphore()
    for where in partners:
        pl.semaphore_signal(barrier, inc=1, device_id=at(**where), device_id_type=MESH)
    wgu[H:HP, :] = jnp.zeros((HP - H, R), BF16)
    wgu[HP + H :, :] = jnp.zeros((HP - H, R), BF16)
    wd[H:, :] = jnp.zeros((HP - H, R), BF16)
    pl.semaphore_wait(barrier, len(partners))

    y32 = pl.multiple_of(y * 32, 32)

    def shard(d):
        return (zl + d + 8) % 8

    def span(piece, half):
        if piece < 2:
            return pl.ds(piece * 64, 64)
        if half is None:
            return pl.ds(y32, 32)
        return pl.ds(pl.multiple_of(y * 32 + half * 16, 16), 16)

    ring = {}

    def ring_send(k, piece):
        for way in (1, -1):
            half = None
            if k == 3:
                half = 0 if way == 1 else 1
                if piece < 2 and piece != half:
                    continue
            rows = span(piece, half)
            buf = gg if piece == 2 else xg
            dst = buf.at[shard(-way * k), rows]
            src = (g_hbm if piece == 2 else x_hbm).at[rows] if k == 0 else dst
            ring[k + 1, piece, way] = send(src, dst, dict(dz=way))

    ycopies, ccopies, xcopies, hcopies, dcopies, icopies, zcopies = ({} for _ in range(7))

    def start():
        for piece in (0, 2, 1):
            ring_send(0, piece)
        for copy in local:
            copy.wait()

    def arrive(k, piece):
        for way in (1, -1):
            if (k, piece, way) in ring:
                ring[k, piece, way].wait_recv()
        if k < 4:
            ring_send(k, piece)
        if piece == 2:
            for d in CHUNKS[k]:
                quarter = gg.at[shard(d), pl.ds(y32, 32)]
                for dy in (1, 2, 3):
                    ycopies[k, d, dy] = send(quarter, quarter, dict(dy=dy))

    def project(k, which):
        if which == 1 and k > 0:
            for d in CHUNKS[k]:
                for dy in (1, 2, 3):
                    ycopies[k, d, dy].wait_recv()
        w, buf = (wd, gg) if which else (wgu, xg)
        cols = slice(2 * HP, 3 * HP) if which else slice(0, 2 * HP)
        for i, d in enumerate(CHUNKS[k]):
            part = lax.dot_general(
                buf[shard(d)], w[...], (((1,), (1,)), ((), ())), preferred_element_type=F32
            ).reshape(2, 4, K, -1)
            pf[k][:, :, i, :, cols] = part
            pb[k][:, :, i, :, cols] = part.astype(BF16)
        if which:
            ccopies[k] = send(pb[k].at[1 - c], cr[k], dict(dc=1))

    def join_cores(k):
        ccopies[k].wait_recv()
        total = pf[k][c] + cr[k][...].astype(F32)
        sf[k][...] = total
        xs[k][...] = total.astype(BF16)
        for dx in (2, 1, 3):
            xcopies[k, dx] = send(xs[k].at[(x + dx) % 4], xr[k].at[dx - 1], dict(dx=dx))

    def activate(k):
        for dx in (1, 2, 3):
            xcopies[k, dx].wait_recv()
        total = sf[k][x]
        for dx in (1, 2, 3):
            total = total + xr[k][dx - 1].astype(F32)
        gate, up, grad = total[..., :HP], total[..., HP : 2 * HP], total[..., 2 * HP :]
        sig = jax.nn.sigmoid(gate)
        silu = gate * sig
        hg[k][c, x, :, :, 0:HP] = (silu * up).astype(BF16)
        hg[k][c, x, :, :, HP : 2 * HP] = (grad * up * sig * (1.0 + gate * (1.0 - sig))).astype(BF16)
        hg[k][c, x, :, :, 2 * HP :] = (grad * silu).astype(BF16)
        mine = hg[k].at[c, x]
        for dx in (2, 1, 3):
            hcopies[k, dx] = send(mine, mine, dict(dx=dx))

    def share(k):
        for dx in (1, 2, 3):
            hcopies[k, dx].wait_recv()
        dcopies[k] = send(hg[k].at[c], hg[k].at[c], dict(dc=1))

    def backward(k):
        dcopies[k].wait_recv()
        n = len(CHUNKS[k])
        delta = hg[k][..., HP:].reshape(n * T, 2 * HP)
        part = jnp.dot(delta, wgu[...], preferred_element_type=F32).reshape(2, 4, n, K, R)
        for h in range(2):
            igf[k][:, h] = part[h]
            igb[k][:, h] = part[h].astype(BF16)
        for dy in (2, 1, 3):
            icopies[k, dy] = send(igb[k].at[(y + dy) % 4], yr[k].at[dy - 1], dict(dy=dy))

    def weights(k):
        for i, d in enumerate(CHUNKS[k]):
            act = hg[k][:, :, i].reshape(T, 3 * HP)
            for cols, buf in ((slice(0, HP), gg), (slice(HP, 3 * HP), xg)):
                part = lax.dot_general(
                    act[:, cols], buf[shard(d)], (((0,), (0,)), ((), ())), preferred_element_type=F32
                )
                if k == 0:
                    acc[cols, :] = part
                else:
                    acc[cols, :] += part

    def spread(k):
        for dy in (1, 2, 3):
            icopies[k, dy].wait_recv()
        total = igf[k][y]
        for dy in (1, 2, 3):
            total = total + yr[k][dy - 1].astype(F32)
        zs[k][...] = total.astype(BF16)
        if k == 0:
            zf[...] = total[:, 0]
        for i, d in enumerate(CHUNKS[k]):
            for e in ((d + 8) % 16, d % 16):
                if e:
                    high = ((z + e) % 16) // 8
                    zcopies[e] = send(zs[k].at[high, i], zr.at[e - 1], dict(dz=e))

    def finish():
        total = zf[zh]
        for e in sorted(zcopies):
            zcopies[e].wait_recv()
        for e in sorted(zcopies):
            total = total + zr[e - 1].astype(F32)
        ig_out[...] = total.astype(BF16)

    def write():
        dg_out[...] = acc[0:H, :].astype(BF16)
        gg_out[...] = acc[HP : HP + H, :].astype(BF16)
        ug_out[...] = acc[2 * HP : 2 * HP + H, :].astype(BF16)

    start()
    project(0, 0)
    project(0, 1)
    last = len(CHUNKS) - 1
    for t in range(1, last + 7):
        if t <= last:
            arrive(t, 0)
            arrive(t, 2)
            arrive(t, 1)
        for stage, lag in ((spread, 6), (backward, 5), (share, 4), (activate, 3), (join_cores, 2)):
            k = t - lag
            if 0 <= k <= last:
                stage(k)
        if 0 <= t - 1 <= last and t > 1:
            project(t - 1, 0)
            project(t - 1, 1)
        k = t - 5
        if 0 <= k <= last:
            weights(k)
        if k == last:
            write()
    finish()
    for copy in sent:
        copy.wait_send()


def body(inputs, out_grad, gate_weight, up_weight, down_weight):
    any_spec = pl.BlockSpec(memory_space=pl.ANY)
    vmem_spec = pl.BlockSpec(memory_space=pltpu.VMEM)
    sizes = [len(c) for c in CHUNKS]

    def each(make):
        return [pltpu.VMEM(*make(n)) for n in sizes]

    wide = 3 * HP
    bufs = (
        each(lambda n: ((2, 4, n, K, wide), F32))
        + each(lambda n: ((2, 4, n, K, wide), BF16))
        + each(lambda n: ((4, n, K, wide), BF16))
        + each(lambda n: ((4, n, K, wide), F32))
        + each(lambda n: ((4, n, K, wide), BF16))
        + each(lambda n: ((3, n, K, wide), BF16))
        + each(lambda n: ((2, 4, n, K, wide), BF16))
        + each(lambda n: ((4, 2, n, K, R), F32))
        + each(lambda n: ((4, 2, n, K, R), BF16))
        + each(lambda n: ((3, 2, n, K, R), BF16))
        + each(lambda n: ((2, n, K, R), BF16))
    )
    return pl.pallas_call(
        kernel,
        out_shape=(
            jax.ShapeDtypeStruct((K, R), BF16),
            jax.ShapeDtypeStruct((H, R), BF16),
            jax.ShapeDtypeStruct((H, R), BF16),
            jax.ShapeDtypeStruct((H, R), BF16),
        ),
        in_specs=[any_spec] * 5,
        out_specs=(vmem_spec,) * 4,
        scratch_shapes=[
            pltpu.VMEM((8, T, R), BF16),
            pltpu.VMEM((8, T, R), BF16),
            pltpu.VMEM((2 * HP, R), BF16),
            pltpu.VMEM((HP, R), BF16),
            pltpu.VMEM((3 * HP, R), F32),
            pltpu.VMEM((15, K, R), BF16),
            pltpu.VMEM((2, K, R), F32),
            pltpu.SemaphoreType.DMA((5,)),
            pltpu.SemaphoreType.DMA((N_SEM,)),
            pltpu.SemaphoreType.DMA((N_SEM,)),
        ]
        + bufs,
        compiler_params=pltpu.CompilerParams(
            collective_id=0, has_side_effects=True, vmem_limit_bytes=56 * 2**20
        ),
        name="swiglu_backward",
    )(inputs, out_grad, gate_weight, up_weight, down_weight)


def solution(mesh):
    return jax.shard_map(
        body,
        mesh=mesh,
        in_specs=(
            P("dep", "inp"),
            P("dep", "inp"),
            P(("out", "dep"), "inp"),
            P(("out", "dep"), "inp"),
            P(("out", "dep"), "inp"),
        ),
        out_specs=(
            P(("dep", "out"), "inp"),
            P(("out", "dep"), "inp"),
            P(("out", "dep"), "inp"),
            P(("out", "dep"), "inp"),
        ),
        check_vma=False,
    )
```

```python
import functools

import jax
import jax.numpy as jnp
from jax import lax
from jax.experimental import pallas as pl
from jax.experimental.pallas import tpu as pltpu
from jax.sharding import PartitionSpec as P

MESH = pl.DeviceIdType.MESH
BF16, F32 = jnp.bfloat16, jnp.float32
T, R, H, HP, K = 128, 512, 224, 256, 16
CHUNKS = ((0,), (-1,), (1,), (-2,), (2,), (-3,), (3,), (4,))
PIECES = (2, 0, 1)
N_SEM = 160


ORDER = (
    ("arrive", 1, 2), ("project_x", 0), ("project_g", 0), ("arrive", 1, 0), ("join_cores", 0),
    ("arrive", 1, 1), ("project_x", 2), ("arrive", 2, 2), ("project_x", 1), ("project_g", 1),
    ("arrive", 2, 0), ("join_cores", 1), ("activate", 0), ("project_g", 2), ("arrive", 2, 1),
    ("project_x", 3), ("arrive", 3, 2), ("project_g", 3), ("join_cores", 2), ("project_x", 4),
    ("join_cores", 3), ("project_g", 4), ("arrive", 3, 0), ("activate", 1), ("arrive", 3, 1),
    ("join_cores", 4), ("share", 0), ("arrive", 4, 2), ("project_x", 5), ("project_g", 5), ("activate", 2),
    ("project_x", 6), ("project_g", 6), ("activate", 3), ("arrive", 4, 1), ("arrive", 4, 0), ("backward", 0),
    ("join_cores", 6), ("project_x", 7), ("join_cores", 5), ("project_g", 7), ("share", 1), ("activate", 4),
    ("join_cores", 7), ("share", 3), ("backward", 1), ("activate", 6), ("share", 2), ("backward", 3),
    ("spread", 0), ("activate", 5), ("backward", 2), ("share", 4), ("activate", 7), ("backward", 4),
    ("weights", 4), ("share", 6), ("spread", 1), ("weights", 0), ("share", 5), ("backward", 6), ("spread", 3),
    ("backward", 5), ("spread", 2), ("share", 7), ("spread", 4), ("backward", 7), ("weights", 1),
    ("weights", 3), ("weights", 7), ("spread", 6), ("weights", 6), ("spread", 5), ("weights", 2),
    ("weights", 5), ("spread", 7), ("write", 0), ("finish", 0),
)


def kernel(
    x_hbm, g_hbm, wg_hbm, wu_hbm, wd_hbm, ig_out, gg_out, ug_out, dg_out,
    xg, gg, wgu, wd, acc, zr, zf, ig_buf, wbuf, local_sem, store_sem, send_sem, recv_sem, relay, *bufs,
):
    inp, out, zl = lax.axis_index("inp"), lax.axis_index("out"), lax.axis_index("dep")
    x, c, y, zh = inp // 2, inp % 2, out % 4, out // 4
    z = zh * 8 + zl

    def at(dx=0, dc=0, dy=0, dz=0):
        zz = (z + dz) % 16
        return {
            "inp": ((x + dx) % 4) * 2 + (c + dc) % 2,
            "out": (zz // 8) * 4 + (y + dy) % 4,
            "dep": zz % 8,
        }

    partners = [dict(dc=1)] + [dict(dx=d) for d in (1, 2, 3)]
    partners += [dict(dy=d) for d in (1, 2, 3)] + [dict(dz=d) for d in (1, 15)]

    pf, cr, sf, xs, xr, hg, igf, igb, yr, zs = (
        bufs[i * len(CHUNKS) : (i + 1) * len(CHUNKS)] for i in range(10)
    )
    count = iter(range(N_SEM))
    sent = []

    def send(src, dst, where):
        i = next(count)
        copy = pltpu.make_async_remote_copy(
            src_ref=src, dst_ref=dst, send_sem=send_sem.at[i], recv_sem=recv_sem.at[i],
            device_id=at(**where), device_id_type=MESH,
        )
        copy.start()
        sent.append(copy)
        return copy

    stored = []

    def store(src, dst):
        copy = pltpu.make_async_copy(src, dst, store_sem.at[len(stored)])
        copy.start()
        stored.append(copy)

    local = []

    def fetch(src, dst):
        copy = pltpu.make_async_copy(src, dst, local_sem.at[len(local)])
        copy.start()
        local.append(copy)

    fetch(x_hbm, xg.at[zl])
    fetch(wg_hbm, wgu.at[pl.ds(0, H)])
    fetch(wu_hbm, wgu.at[pl.ds(HP, H)])
    fetch(wd_hbm, wd.at[pl.ds(0, H)])
    fetch(g_hbm, gg.at[zl])

    barrier = pltpu.get_barrier_semaphore()
    for where in partners:
        pl.semaphore_signal(barrier, inc=1, device_id=at(**where), device_id_type=MESH)
    wgu[H:HP, :] = jnp.zeros((HP - H, R), BF16)
    wgu[HP + H :, :] = jnp.zeros((HP - H, R), BF16)
    wd[H:, :] = jnp.zeros((HP - H, R), BF16)
    pl.semaphore_wait(barrier, len(partners))

    y32 = pl.multiple_of(y * 32, 32)

    def shard(d):
        return (zl + d + 8) % 8

    def span(piece, half):
        if piece < 2:
            return pl.ds(piece * 64, 64)
        if half is None:
            return pl.ds(y32, 32)
        return pl.ds(pl.multiple_of(y * 32 + half * 16, 16), 16)

    ring = {}

    def ring_send(k, piece):
        for way in (1, -1):
            half = None
            if k == 3:
                half = 0 if way == 1 else 1
                if piece < 2 and piece != half:
                    continue
            rows = span(piece, half)
            buf = gg if piece == 2 else xg
            dst = buf.at[shard(-way * k), rows]
            src = (g_hbm if piece == 2 else x_hbm).at[rows] if k == 0 else dst
            ring[k + 1, piece, way] = send(src, dst, dict(dz=way))

    weighed, spreads = [], []
    ycopies, ccopies, xcopies, hcopies, dcopies, icopies, zcopies = ({} for _ in range(7))

    def start():
        for piece in PIECES:
            ring_send(0, piece)
        for copy in local:
            copy.wait()

    def arrive(k, piece):
        for way in (1, -1):
            if (k, piece, way) in ring:
                ring[k, piece, way].wait_recv()
        if k < 4:
            ring_send(k, piece)
        elif piece == 2:
            for way in (4, 12):
                pl.semaphore_signal(relay, inc=1, device_id=at(dz=way), device_id_type=MESH)
        if piece == 2:
            for d in (-k, k) if k < 4 else (4,):
                quarter = gg.at[shard(d), pl.ds(y32, 32)]
                for dy in (1, 2, 3):
                    ycopies[d, dy] = send(quarter, quarter, dict(dy=dy))

    def project(k, which):
        if which == 1 and k > 0:
            for d in CHUNKS[k]:
                for dy in (1, 2, 3):
                    ycopies[d, dy].wait_recv()
        w, buf = (wd, gg) if which else (wgu, xg)
        cols = slice(2 * HP, 3 * HP) if which else slice(0, 2 * HP)
        for i, d in enumerate(CHUNKS[k]):
            part = lax.dot_general(
                buf[shard(d)], w[...], (((1,), (1,)), ((), ())), preferred_element_type=F32
            ).reshape(2, 4, K, -1)
            pf[k][:, :, i, :, cols] = part
        if which:
            ccopies[k] = send(pf[k].at[1 - c], cr[k], dict(dc=1))

    def join_cores(k):
        ccopies[k].wait_recv()
        total = pf[k][c] + cr[k][...]
        sf[k][...] = total
        xs[k][...] = total.astype(BF16)
        for dx in (2, 1, 3):
            xcopies[k, dx] = send(xs[k].at[(x + dx) % 4], xr[k].at[dx - 1], dict(dx=dx))

    def activate(k):
        for dx in (1, 2, 3):
            xcopies[k, dx].wait_recv()
        total = sf[k][x]
        for dx in (1, 2, 3):
            total = total + xr[k][dx - 1].astype(F32)
        gate, up, grad = total[..., :HP], total[..., HP : 2 * HP], total[..., 2 * HP :]
        sig = jax.nn.sigmoid(gate)
        silu = gate * sig
        hg[k][c, x, :, :, 0:HP] = (silu * up).astype(BF16)
        hg[k][c, x, :, :, HP : 2 * HP] = (grad * up * sig * (1.0 + gate * (1.0 - sig))).astype(BF16)
        hg[k][c, x, :, :, 2 * HP :] = (grad * silu).astype(BF16)
        mine = hg[k].at[c, x]
        for dx in (2, 1, 3):
            hcopies[k, dx] = send(mine, mine, dict(dx=dx))

    def share(k):
        for dx in (1, 2, 3):
            hcopies[k, dx].wait_recv()
        dcopies[k] = send(hg[k].at[c], hg[k].at[c], dict(dc=1))

    def backward(k):
        dcopies[k].wait_recv()
        n = len(CHUNKS[k])
        delta = hg[k][..., HP:].reshape(n * T, 2 * HP)
        part = jnp.dot(delta, wgu[...], preferred_element_type=F32).reshape(2, 4, n, K, R)
        for h in range(2):
            igf[k][:, h] = part[h]
            igb[k][:, h] = part[h].astype(BF16)
        for dy in (2, 1, 3):
            icopies[k, dy] = send(igb[k].at[(y + dy) % 4], yr[k].at[dy - 1], dict(dy=dy))

    def weights(k):
        for i, d in enumerate(CHUNKS[k]):
            act = hg[k][:, :, i].reshape(T, 3 * HP)
            for cols, buf in ((slice(0, HP), gg), (slice(HP, 3 * HP), xg)):
                part = lax.dot_general(
                    act[:, cols], buf[shard(d)], (((0,), (0,)), ((), ())), preferred_element_type=F32
                )
                if not weighed:
                    acc[cols, :] = part
                else:
                    acc[cols, :] += part
        weighed.append(k)

    def spread(k):
        for dy in (1, 2, 3):
            icopies[k, dy].wait_recv()
        total = igf[k][y]
        for dy in (1, 2, 3):
            total = total + yr[k][dy - 1].astype(F32)
        zs[k][...] = total.astype(BF16)
        if not spreads:
            pl.semaphore_wait(relay, 2)
        spreads.append(k)
        if k == 0:
            zf[...] = total[:, 0]
        for i, d in enumerate(CHUNKS[k]):
            for e in ((d + 8) % 16, d % 16):
                if e:
                    high = ((z + e) % 16) // 8
                    zcopies[e] = send(zs[k].at[high, i], zr.at[e - 1], dict(dz=e))

    def finish():
        total = zf[zh]
        for e in sorted(zcopies):
            zcopies[e].wait_recv()
        for e in sorted(zcopies):
            total = total + zr[e - 1].astype(F32)
        ig_buf[...] = total.astype(BF16)
        store(ig_buf, ig_out)

    def write():
        for i, result in enumerate((dg_out, gg_out, ug_out)):
            wbuf[i] = acc[i * HP : i * HP + H, :].astype(BF16)
            store(wbuf.at[i], result)

    start()
    steps = dict(
        arrive=arrive, project_x=lambda k: project(k, 0), project_g=lambda k: project(k, 1),
        join_cores=join_cores, activate=activate, share=share, backward=backward,
        weights=weights, spread=spread, write=lambda k: write(), finish=lambda k: finish(),
    )
    for name, *where in ORDER:
        steps[name](*where)
    for copy in sent:
        copy.wait_send()
    for copy in stored:
        copy.wait()


def land(*refs):
    sources, results, held, sem_in, sem_out = refs[:4], refs[4:8], refs[8:12], refs[12], refs[13]
    loads = [pltpu.make_async_copy(sources[i], held[i], sem_in.at[i]) for i in range(4)]
    stores = [pltpu.make_async_copy(held[i], results[i], sem_out.at[i]) for i in range(4)]
    for load in loads:
        load.start()
    for load, store in zip(loads, stores):
        load.wait()
        store.start()
    for store in stores:
        store.wait()


def body(inputs, out_grad, gate_weight, up_weight, down_weight):
    any_spec = pl.BlockSpec(memory_space=pl.ANY)
    sizes = [len(c) for c in CHUNKS]

    def each(make):
        return [pltpu.VMEM(*make(n)) for n in sizes]

    wide = 3 * HP
    bufs = (
        each(lambda n: ((2, 4, n, K, wide), F32))
        + each(lambda n: ((4, n, K, wide), F32))
        + each(lambda n: ((4, n, K, wide), F32))
        + each(lambda n: ((4, n, K, wide), BF16))
        + each(lambda n: ((3, n, K, wide), BF16))
        + each(lambda n: ((2, 4, n, K, wide), BF16))
        + each(lambda n: ((4, 2, n, K, R), F32))
        + each(lambda n: ((4, 2, n, K, R), BF16))
        + each(lambda n: ((3, 2, n, K, R), BF16))
        + each(lambda n: ((2, n, K, R), BF16))
    )
    parts = pl.pallas_call(
        kernel,
        out_shape=(
            jax.ShapeDtypeStruct((K, R), BF16),
            jax.ShapeDtypeStruct((H, R), BF16),
            jax.ShapeDtypeStruct((H, R), BF16),
            jax.ShapeDtypeStruct((H, R), BF16),
        ),
        in_specs=[any_spec] * 5,
        out_specs=(any_spec,) * 4,
        scratch_shapes=[
            pltpu.VMEM((8, T, R), BF16),
            pltpu.VMEM((8, T, R), BF16),
            pltpu.VMEM((2 * HP, R), BF16),
            pltpu.VMEM((HP, R), BF16),
            pltpu.VMEM((3 * HP, R), F32),
            pltpu.VMEM((15, K, R), BF16),
            pltpu.VMEM((2, K, R), F32),
            pltpu.VMEM((K, R), BF16),
            pltpu.VMEM((3, H, R), BF16),
            pltpu.SemaphoreType.DMA((5,)),
            pltpu.SemaphoreType.DMA((4,)),
            pltpu.SemaphoreType.DMA((N_SEM,)),
            pltpu.SemaphoreType.DMA((N_SEM,)),
            pltpu.SemaphoreType.REGULAR,
        ]
        + bufs,
        compiler_params=pltpu.CompilerParams(
            collective_id=0, has_side_effects=True, vmem_limit_bytes=56 * 2**20
        ),
        name="swiglu_backward",
    )(inputs, out_grad, gate_weight, up_weight, down_weight)
    return tuple(
        pl.pallas_call(
            land,
            out_shape=tuple(jax.ShapeDtypeStruct(p.shape, p.dtype) for p in parts),
            in_specs=[any_spec] * 4,
            out_specs=(any_spec,) * 4,
            scratch_shapes=[pltpu.VMEM(p.shape, p.dtype) for p in parts]
            + [pltpu.SemaphoreType.DMA((4,)), pltpu.SemaphoreType.DMA((4,))],
            name="land",
        )(*parts)
    )


def solution(mesh):
    return jax.shard_map(
        body,
        mesh=mesh,
        in_specs=(
            P("dep", "inp"),
            P("dep", "inp"),
            P(("out", "dep"), "inp"),
            P(("out", "dep"), "inp"),
            P(("out", "dep"), "inp"),
        ),
        out_specs=(
            P(("dep", "out"), "inp"),
            P(("out", "dep"), "inp"),
            P(("out", "dep"), "inp"),
            P(("out", "dep"), "inp"),
        ),
        check_vma=False,
    )
```

```python
import functools

import jax
import jax.numpy as jnp
from jax import lax
from jax.experimental import pallas as pl
from jax.experimental.pallas import tpu as pltpu
from jax.sharding import PartitionSpec as P

MESH = pl.DeviceIdType.MESH
BF16, F32 = jnp.bfloat16, jnp.float32
T, R, H, HP, K = 128, 512, 224, 256, 16
CHUNKS = ((0,), (-1,), (1,), (-2,), (2,), (-3,), (3,), (4,))
PIECES = (2, 0, 1)
N_SEM = 160


ORDER = (
    ("project_x", 0), ("arrive", 1, 2, 1), ("arrive", 1, 2, -1), ("project_g", 0), ("arrive", 1, 0, 1),
    ("arrive", 1, 0, -1), ("join_cores", 0), ("arrive", 1, 1, 1), ("arrive", 1, 1, -1), ("project_x", 1),
    ("arrive", 2, 2, 1), ("arrive", 2, 2, -1), ("project_x", 2), ("project_g", 1), ("arrive", 2, 0, 1),
    ("arrive", 2, 0, -1), ("project_g", 2), ("join_cores", 1), ("activate", 0), ("arrive", 2, 1, 1),
    ("arrive", 2, 1, -1), ("project_x", 3), ("join_cores", 2), ("project_g", 3), ("arrive", 3, 2, 1),
    ("arrive", 3, 2, -1), ("project_x", 4), ("join_cores", 3), ("project_g", 4), ("arrive", 3, 0, 1),
    ("arrive", 3, 0, -1), ("activate", 1), ("arrive", 3, 1, 1), ("arrive", 3, 1, -1), ("project_x", 5),
    ("join_cores", 4), ("arrive", 4, 2, 1), ("arrive", 4, 2, -1), ("activate", 2), ("project_x", 6),
    ("project_g", 5), ("activate", 3), ("share", 0), ("project_g", 6), ("join_cores", 5), ("arrive", 4, 0, 1),
    ("arrive", 4, 1, -1), ("project_x", 7), ("join_cores", 6), ("project_g", 7), ("share", 1),
    ("backward", 0), ("share", 2), ("activate", 4), ("join_cores", 7), ("backward", 1), ("share", 3),
    ("backward", 2), ("activate", 5), ("backward", 3), ("activate", 6), ("share", 4), ("spread", 0),
    ("activate", 7), ("backward", 4), ("share", 5), ("spread", 1), ("weights", 1), ("spread", 2),
    ("share", 6), ("backward", 5), ("spread", 3), ("backward", 6), ("share", 7), ("weights", 5),
    ("spread", 4), ("backward", 7), ("weights", 0), ("spread", 5), ("weights", 7), ("weights", 3),
    ("spread", 6), ("weights", 6), ("spread", 7), ("finish", 0), ("weights", 2), ("weights", 4), ("write", 0),
)


def kernel(
    x_hbm, g_hbm, wg_hbm, wu_hbm, wd_hbm, ig_out, gg_out, ug_out, dg_out,
    xg, gg, wgu, wd, acc, zr, zf, ig_buf, wbuf, local_sem, store_sem, send_sem, recv_sem, relay, *bufs,
):
    inp, out, zl = lax.axis_index("inp"), lax.axis_index("out"), lax.axis_index("dep")
    x, c, y, zh = inp // 2, inp % 2, out % 4, out // 4
    z = zh * 8 + zl

    def at(dx=0, dc=0, dy=0, dz=0):
        zz = (z + dz) % 16
        return {
            "inp": ((x + dx) % 4) * 2 + (c + dc) % 2,
            "out": (zz // 8) * 4 + (y + dy) % 4,
            "dep": zz % 8,
        }

    partners = [dict(dz=1), dict(dz=15), dict(dc=1)]
    partners += [dict(dx=d) for d in (1, 2, 3)] + [dict(dy=d) for d in (1, 2, 3)]

    pf, cr, sf, xs, xr, hg, igf, igb, yr, zs = (
        bufs[i * len(CHUNKS) : (i + 1) * len(CHUNKS)] for i in range(10)
    )
    count = iter(range(N_SEM))
    sent = []

    def send(src, dst, where):
        i = next(count)
        copy = pltpu.make_async_remote_copy(
            src_ref=src, dst_ref=dst, send_sem=send_sem.at[i], recv_sem=recv_sem.at[i],
            device_id=at(**where), device_id_type=MESH,
        )
        copy.start()
        sent.append(copy)
        return copy

    stored = []

    def store(src, dst):
        copy = pltpu.make_async_copy(src, dst, store_sem.at[len(stored)])
        copy.start()
        stored.append(copy)

    local = []

    def fetch(src, dst):
        copy = pltpu.make_async_copy(src, dst, local_sem.at[len(local)])
        copy.start()
        local.append(copy)

    barrier = pltpu.get_barrier_semaphore()
    for where in partners:
        pl.semaphore_signal(barrier, inc=1, device_id=at(**where), device_id_type=MESH)
    fetch(x_hbm, xg.at[zl])
    fetch(wg_hbm, wgu.at[pl.ds(0, H)])
    fetch(wu_hbm, wgu.at[pl.ds(HP, H)])
    fetch(wd_hbm, wd.at[pl.ds(0, H)])
    fetch(g_hbm, gg.at[zl])
    wgu[H:HP, :] = jnp.zeros((HP - H, R), BF16)
    wgu[HP + H :, :] = jnp.zeros((HP - H, R), BF16)
    wd[H:, :] = jnp.zeros((HP - H, R), BF16)
    pl.semaphore_wait(barrier, len(partners))

    y32 = pl.multiple_of(y * 32, 32)

    def shard(d):
        return (zl + d + 8) % 8

    def span(piece, half):
        if piece < 2:
            return pl.ds(piece * 64, 64)
        if half is None:
            return pl.ds(y32, 32)
        return pl.ds(pl.multiple_of(y * 32 + half * 16, 16), 16)

    ring = {}

    def ring_send(k, piece, way):
        half = None
        if k == 3:
            half = 0 if way == 1 else 1
            if piece < 2 and piece != half:
                return
        rows = span(piece, half)
        buf = gg if piece == 2 else xg
        dst = buf.at[shard(-way * k), rows]
        src = (g_hbm if piece == 2 else x_hbm).at[rows] if k == 0 else dst
        ring[k + 1, piece, way] = send(src, dst, dict(dz=way))

    weighed, spreads = [], []
    ycopies, ccopies, xcopies, hcopies, dcopies, icopies, zcopies = ({} for _ in range(7))

    def start():
        for piece in PIECES:
            for way in (1, -1):
                ring_send(0, piece, way)
        for copy in local:
            copy.wait()

    def arrive(k, piece, way):
        ring[k, piece, way].wait_recv()
        if k < 4:
            ring_send(k, piece, way)
        if piece == 2 and (k < 4 or way == -1):
            d = -way * k if k < 4 else 4
            quarter = gg.at[shard(d), pl.ds(y32, 32)]
            for dy in (2, 1, 3):
                ycopies[d, dy] = send(quarter, quarter, dict(dy=dy))
        if k == 4 and piece == 2 and way == -1:
            for far in (4, 12):
                pl.semaphore_signal(relay, inc=1, device_id=at(dz=far), device_id_type=MESH)

    def project(k, which):
        if which == 1 and k > 0:
            for d in CHUNKS[k]:
                for dy in (1, 2, 3):
                    ycopies[d, dy].wait_recv()
        w, buf = (wd, gg) if which else (wgu, xg)
        cols = slice(2 * HP, 3 * HP) if which else slice(0, 2 * HP)
        for i, d in enumerate(CHUNKS[k]):
            part = lax.dot_general(
                buf[shard(d)], w[...], (((1,), (1,)), ((), ())), preferred_element_type=F32
            ).reshape(2, 4, K, -1)
            pf[k][:, :, i, :, cols] = part
        if which:
            ccopies[k] = send(pf[k].at[1 - c], cr[k], dict(dc=1))

    def join_cores(k):
        ccopies[k].wait_recv()
        total = pf[k][c] + cr[k][...]
        sf[k][...] = total
        xs[k][...] = total.astype(BF16)
        for dx in (2, 1, 3):
            xcopies[k, dx] = send(xs[k].at[(x + dx) % 4], xr[k].at[dx - 1], dict(dx=dx))

    def activate(k):
        for dx in (1, 2, 3):
            xcopies[k, dx].wait_recv()
        total = sf[k][x]
        for dx in (1, 2, 3):
            total = total + xr[k][dx - 1].astype(F32)
        gate, up, grad = total[..., :HP], total[..., HP : 2 * HP], total[..., 2 * HP :]
        sig = jax.nn.sigmoid(gate)
        silu = gate * sig
        hg[k][c, x, :, :, 0:HP] = (silu * up).astype(BF16)
        hg[k][c, x, :, :, HP : 2 * HP] = (grad * up * sig * (1.0 + gate * (1.0 - sig))).astype(BF16)
        hg[k][c, x, :, :, 2 * HP :] = (grad * silu).astype(BF16)
        mine = hg[k].at[c, x]
        for dx in (2, 1, 3):
            hcopies[k, dx] = send(mine, mine, dict(dx=dx))

    def share(k):
        for dx in (1, 2, 3):
            hcopies[k, dx].wait_recv()
        dcopies[k] = send(hg[k].at[c], hg[k].at[c], dict(dc=1))

    def backward(k):
        dcopies[k].wait_recv()
        n = len(CHUNKS[k])
        delta = hg[k][..., HP:].reshape(n * T, 2 * HP)
        part = jnp.dot(delta, wgu[...], preferred_element_type=F32).reshape(2, 4, n, K, R)
        for h in range(2):
            igf[k][:, h] = part[h]
            igb[k][:, h] = part[h].astype(BF16)
        for dy in (2, 1, 3):
            icopies[k, dy] = send(igb[k].at[(y + dy) % 4], yr[k].at[dy - 1], dict(dy=dy))

    def weights(k):
        for i, d in enumerate(CHUNKS[k]):
            act = hg[k][:, :, i].reshape(T, 3 * HP)
            for cols, buf in ((slice(0, HP), gg), (slice(HP, 3 * HP), xg)):
                part = lax.dot_general(
                    act[:, cols], buf[shard(d)], (((0,), (0,)), ((), ())), preferred_element_type=F32
                )
                if not weighed:
                    acc[cols, :] = part
                else:
                    acc[cols, :] += part
        weighed.append(k)

    def spread(k):
        for dy in (1, 2, 3):
            icopies[k, dy].wait_recv()
        total = igf[k][y]
        for dy in (1, 2, 3):
            total = total + yr[k][dy - 1].astype(F32)
        zs[k][...] = total.astype(BF16)
        if not spreads:
            pl.semaphore_wait(relay, 2)
        spreads.append(k)
        if k == 0:
            zf[...] = total[:, 0]
        for i, d in enumerate(CHUNKS[k]):
            for e in ((d + 8) % 16, d % 16):
                if e:
                    high = ((z + e) % 16) // 8
                    zcopies[e] = send(zs[k].at[high, i], zr.at[e - 1], dict(dz=e))

    def finish():
        for copy in sent:
            if all(copy is not q for q in zcopies.values()):
                copy.wait_send()
        total = zf[zh]
        for e in sorted(zcopies):
            zcopies[e].wait_recv()
        for e in sorted(zcopies):
            total = total + zr[e - 1].astype(F32)
        ig_buf[...] = total.astype(BF16)
        store(ig_buf, ig_out)

    def write():
        for i, result in enumerate((dg_out, gg_out, ug_out)):
            wbuf[i] = acc[i * HP : i * HP + H, :].astype(BF16)
            store(wbuf.at[i], result)

    start()
    steps = dict(
        arrive=arrive, project_x=lambda k: project(k, 0), project_g=lambda k: project(k, 1),
        join_cores=join_cores, activate=activate, share=share, backward=backward,
        weights=weights, spread=spread, write=lambda k: write(), finish=lambda k: finish(),
    )
    for name, *where in ORDER:
        steps[name](*where)
    for copy in zcopies.values():
        copy.wait_send()
    for copy in stored:
        copy.wait()


def land(*refs):
    sources, results, held, sem_in, sem_out = refs[:4], refs[4:8], refs[8:12], refs[12], refs[13]
    loads = [pltpu.make_async_copy(sources[i], held[i], sem_in.at[i]) for i in range(4)]
    stores = [pltpu.make_async_copy(held[i], results[i], sem_out.at[i]) for i in range(4)]
    for load in loads:
        load.start()
    for load, store in zip(loads, stores):
        load.wait()
        store.start()
    for store in stores:
        store.wait()


def body(inputs, out_grad, gate_weight, up_weight, down_weight):
    any_spec = pl.BlockSpec(memory_space=pl.ANY)
    sizes = [len(c) for c in CHUNKS]

    def each(make):
        return [pltpu.VMEM(*make(n)) for n in sizes]

    wide = 3 * HP
    bufs = (
        each(lambda n: ((2, 4, n, K, wide), F32))
        + each(lambda n: ((4, n, K, wide), F32))
        + each(lambda n: ((4, n, K, wide), F32))
        + each(lambda n: ((4, n, K, wide), BF16))
        + each(lambda n: ((3, n, K, wide), BF16))
        + each(lambda n: ((2, 4, n, K, wide), BF16))
        + each(lambda n: ((4, 2, n, K, R), F32))
        + each(lambda n: ((4, 2, n, K, R), BF16))
        + each(lambda n: ((3, 2, n, K, R), BF16))
        + each(lambda n: ((2, n, K, R), BF16))
    )
    parts = pl.pallas_call(
        kernel,
        out_shape=(
            jax.ShapeDtypeStruct((K, R), BF16),
            jax.ShapeDtypeStruct((H, R), BF16),
            jax.ShapeDtypeStruct((H, R), BF16),
            jax.ShapeDtypeStruct((H, R), BF16),
        ),
        in_specs=[any_spec] * 5,
        out_specs=(any_spec,) * 4,
        scratch_shapes=[
            pltpu.VMEM((8, T, R), BF16),
            pltpu.VMEM((8, T, R), BF16),
            pltpu.VMEM((2 * HP, R), BF16),
            pltpu.VMEM((HP, R), BF16),
            pltpu.VMEM((3 * HP, R), F32),
            pltpu.VMEM((15, K, R), BF16),
            pltpu.VMEM((2, K, R), F32),
            pltpu.VMEM((K, R), BF16),
            pltpu.VMEM((3, H, R), BF16),
            pltpu.SemaphoreType.DMA((5,)),
            pltpu.SemaphoreType.DMA((4,)),
            pltpu.SemaphoreType.DMA((N_SEM,)),
            pltpu.SemaphoreType.DMA((N_SEM,)),
            pltpu.SemaphoreType.REGULAR,
        ]
        + bufs,
        compiler_params=pltpu.CompilerParams(
            collective_id=0, has_side_effects=True, vmem_limit_bytes=56 * 2**20
        ),
        name="swiglu_backward",
    )(inputs, out_grad, gate_weight, up_weight, down_weight)
    return tuple(
        pl.pallas_call(
            land,
            out_shape=tuple(jax.ShapeDtypeStruct(p.shape, p.dtype) for p in parts),
            in_specs=[any_spec] * 4,
            out_specs=(any_spec,) * 4,
            scratch_shapes=[pltpu.VMEM(p.shape, p.dtype) for p in parts]
            + [pltpu.SemaphoreType.DMA((4,)), pltpu.SemaphoreType.DMA((4,))],
            name="land",
        )(*parts)
    )


def solution(mesh):
    return jax.shard_map(
        body,
        mesh=mesh,
        in_specs=(
            P("dep", "inp"),
            P("dep", "inp"),
            P(("out", "dep"), "inp"),
            P(("out", "dep"), "inp"),
            P(("out", "dep"), "inp"),
        ),
        out_specs=(
            P(("dep", "out"), "inp"),
            P(("out", "dep"), "inp"),
            P(("out", "dep"), "inp"),
            P(("out", "dep"), "inp"),
        ),
        check_vma=False,
    )
```

```python
import functools

import jax
import jax.numpy as jnp
from jax import lax
from jax.experimental import pallas as pl
from jax.experimental.pallas import tpu as pltpu
from jax.sharding import PartitionSpec as P

MESH = pl.DeviceIdType.MESH
BF16, F32 = jnp.bfloat16, jnp.float32
T, R, H, HP, K = 128, 512, 224, 256, 16
CHUNKS = ((0,), (-1,), (1,), (-2,), (2,), (-3,), (3,), (4,))
PIECES = (2, 0, 1)
N_SEM = 160


ORDER = (
    ("project_x", 0), ("arrive", 1, 2, 1), ("arrive", 1, 2, -1), ("arrive", 1, 0, 1), ("arrive", 1, 0, -1),
    ("project_g", 0), ("arrive", 1, 1, -1), ("arrive", 1, 1, 1), ("arrive", 2, 2, 1), ("project_x", 1),
    ("join_cores", 0), ("project_g", 1), ("project_x", 2), ("arrive", 2, 2, -1), ("arrive", 2, 0, 1),
    ("arrive", 2, 0, -1), ("project_g", 2), ("join_cores", 1), ("arrive", 2, 1, 1), ("arrive", 2, 1, -1),
    ("project_x", 3), ("join_cores", 2), ("arrive", 3, 2, 1), ("project_g", 3), ("arrive", 3, 2, -1),
    ("activate", 0), ("project_x", 4), ("arrive", 3, 0, 1), ("join_cores", 3), ("activate", 1),
    ("arrive", 3, 0, -1), ("project_g", 4), ("arrive", 3, 1, -1), ("arrive", 4, 2, 1), ("arrive", 4, 2, -1),
    ("activate", 2), ("arrive", 3, 1, 1), ("project_x", 5), ("project_g", 5), ("join_cores", 4),
    ("project_x", 6), ("activate", 3), ("project_g", 6), ("arrive", 4, 0, 1), ("join_cores", 5), ("share", 1),
    ("share", 0), ("arrive", 4, 1, -1), ("project_x", 7), ("project_g", 7), ("join_cores", 6),
    ("backward", 1), ("share", 2), ("backward", 0), ("join_cores", 7), ("activate", 4), ("backward", 2),
    ("activate", 5), ("weights", 1), ("share", 3), ("backward", 3), ("activate", 6), ("spread", 1),
    ("activate", 7), ("weights", 0), ("share", 4), ("backward", 4), ("spread", 0), ("spread", 2),
    ("share", 5), ("backward", 5), ("spread", 3), ("share", 6), ("backward", 6), ("weights", 3), ("share", 7),
    ("weights", 4), ("backward", 7), ("spread", 4), ("weights", 5), ("spread", 5), ("weights", 7),
    ("weights", 6), ("spread", 6), ("spread", 7), ("finish", 0), ("weights", 2), ("write", 0),
)


def kernel(
    x_hbm, g_hbm, wg_hbm, wu_hbm, wd_hbm, ig_out, gg_out, ug_out, dg_out,
    xg, gg, wgu, wd, wother, acc, zr, zsend_sem, zrecv_sem, ig_buf, wbuf, local_sem, store_sem, send_sem, recv_sem, relay, *bufs,
):
    inp, out, zl = lax.axis_index("inp"), lax.axis_index("out"), lax.axis_index("dep")
    x, c, y, zh = inp // 2, inp % 2, out % 4, out // 4
    z = zh * 8 + zl

    def at(dx=0, dc=0, dy=0, dz=0):
        zz = (z + dz) % 16
        return {
            "inp": ((x + dx) % 4) * 2 + (c + dc) % 2,
            "out": (zz // 8) * 4 + (y + dy) % 4,
            "dep": zz % 8,
        }

    partners = [dict(dz=1), dict(dz=15), dict(dc=1)]
    partners += [dict(dx=d) for d in (1, 2, 3)] + [dict(dy=d) for d in (1, 2, 3)]

    pf, cr, sf, xs, xr, hg, igf, igb, yr, zs = (
        bufs[i * len(CHUNKS) : (i + 1) * len(CHUNKS)] for i in range(10)
    )
    count = iter(range(N_SEM))
    sent = []

    def send(src, dst, where):
        i = next(count)
        copy = pltpu.make_async_remote_copy(
            src_ref=src, dst_ref=dst, send_sem=send_sem.at[i], recv_sem=recv_sem.at[i],
            device_id=at(**where), device_id_type=MESH,
        )
        copy.start()
        sent.append(copy)
        return copy

    stored = []

    def store(src, dst):
        copy = pltpu.make_async_copy(src, dst, store_sem.at[len(stored)])
        copy.start()
        stored.append(copy)

    local = []

    def fetch(src, dst):
        copy = pltpu.make_async_copy(src, dst, local_sem.at[len(local)])
        copy.start()
        local.append(copy)

    barrier = pltpu.get_barrier_semaphore()
    for where in partners:
        pl.semaphore_signal(barrier, inc=1, device_id=at(**where), device_id_type=MESH)
    fetch(x_hbm, xg.at[zl])
    fetch(wg_hbm, wgu.at[pl.ds(0, H)])
    fetch(wu_hbm, wgu.at[pl.ds(HP, H)])
    fetch(wd_hbm, wd.at[pl.ds(0, H)])
    fetch(g_hbm, gg.at[zl])
    wgu[H:HP, :] = jnp.zeros((HP - H, R), BF16)
    wgu[HP + H :, :] = jnp.zeros((HP - H, R), BF16)
    wd[H:, :] = jnp.zeros((HP - H, R), BF16)
    pl.semaphore_wait(barrier, len(partners))

    y32 = pl.multiple_of(y * 32, 32)

    def shard(d):
        return (zl + d + 8) % 8

    def span(piece, half):
        if piece < 2:
            return pl.ds(piece * 64, 64)
        if half is None:
            return pl.ds(y32, 32)
        return pl.ds(pl.multiple_of(y * 32 + half * 16, 16), 16)

    ring = {}

    def ring_send(k, piece, way):
        half = None
        if k == 3:
            half = 0 if way == 1 else 1
            if piece < 2 and piece != half:
                return
        rows = span(piece, half)
        buf = gg if piece == 2 else xg
        dst = buf.at[shard(-way * k), rows]
        src = (g_hbm if piece == 2 else x_hbm).at[rows] if k == 0 else dst
        ring[k + 1, piece, way] = send(src, dst, dict(dz=way))

    weighed, spreads, other = [], [], []
    ycopies, ccopies, xcopies, hcopies, dcopies, icopies, zcopies = ({} for _ in range(7))

    def start():
        for piece in PIECES:
            for way in (1, -1):
                ring_send(0, piece, way)
        for copy in local:
            copy.wait()
        other.append(send(wgu, wother, dict(dc=1)))

    def arrive(k, piece, way):
        ring[k, piece, way].wait_recv()
        if k < 4:
            ring_send(k, piece, way)
        if piece == 2 and (k < 4 or way == -1):
            d = -way * k if k < 4 else 4
            quarter = gg.at[shard(d), pl.ds(y32, 32)]
            for dy in (2, 1, 3):
                ycopies[d, dy] = send(quarter, quarter, dict(dy=dy))
        if k == 4 and piece == 2 and way == -1:
            for far in (4, 12):
                pl.semaphore_signal(relay, inc=1, device_id=at(dz=far), device_id_type=MESH)

    def project(k, which):
        if which == 1 and k > 0:
            for d in CHUNKS[k]:
                for dy in (1, 2, 3):
                    ycopies[d, dy].wait_recv()
        w, buf = (wd, gg) if which else (wgu, xg)
        cols = slice(2 * HP, 3 * HP) if which else slice(0, 2 * HP)
        for i, d in enumerate(CHUNKS[k]):
            part = lax.dot_general(
                buf[shard(d)], w[...], (((1,), (1,)), ((), ())), preferred_element_type=F32
            ).reshape(2, 4, K, -1)
            pf[k][:, :, i, :, cols] = part
        if which:
            ccopies[k] = send(pf[k].at[1 - c], cr[k], dict(dc=1))

    def join_cores(k):
        ccopies[k].wait_recv()
        total = pf[k][c] + cr[k][...]
        sf[k][...] = total
        xs[k][...] = total.astype(BF16)
        for dx in (2, 1, 3):
            xcopies[k, dx] = send(xs[k].at[(x + dx) % 4], xr[k].at[dx - 1], dict(dx=dx))

    def activate(k):
        for dx in (1, 2, 3):
            xcopies[k, dx].wait_recv()
        total = sf[k][x]
        for dx in (1, 2, 3):
            total = total + xr[k][dx - 1].astype(F32)
        gate, up, grad = total[..., :HP], total[..., HP : 2 * HP], total[..., 2 * HP :]
        sig = jax.nn.sigmoid(gate)
        silu = gate * sig
        hg[k][c, x, :, :, 0:HP] = (silu * up).astype(BF16)
        hg[k][c, x, :, :, HP : 2 * HP] = (grad * up * sig * (1.0 + gate * (1.0 - sig))).astype(BF16)
        hg[k][c, x, :, :, 2 * HP :] = (grad * silu).astype(BF16)
        mine = hg[k].at[c, x]
        for dx in (2, 1, 3):
            hcopies[k, dx] = send(mine, mine, dict(dx=dx))

    def share(k):
        for dx in (1, 2, 3):
            hcopies[k, dx].wait_recv()
        dcopies[k] = send(hg[k].at[c], hg[k].at[c], dict(dc=1))

    def backward(k):
        if len(other) == 1:
            other[0].wait_recv()
            other.append(k)
        n = len(CHUNKS[k])
        delta = hg[k][c, :, :, :, HP:].reshape(n * T // 2, 2 * HP)
        for f, w in enumerate((wgu, wother)):
            part = jnp.dot(delta, w[...], preferred_element_type=F32).reshape(4, n, K, R)
            igf[k][:, f] = part
            igb[k][:, f] = part.astype(BF16)
        for dy in (2, 1, 3):
            icopies[k, dy] = send(igb[k].at[(y + dy) % 4], yr[k].at[dy - 1], dict(dy=dy))

    def weights(k):
        dcopies[k].wait_recv()
        for i, d in enumerate(CHUNKS[k]):
            act = hg[k][:, :, i].reshape(T, 3 * HP)
            for cols, buf in ((slice(0, HP), gg), (slice(HP, 3 * HP), xg)):
                part = lax.dot_general(
                    act[:, cols], buf[shard(d)], (((0,), (0,)), ((), ())), preferred_element_type=F32
                )
                if not weighed:
                    acc[cols, :] = part
                else:
                    acc[cols, :] += part
        weighed.append(k)

    def spread(k):
        for dy in (1, 2, 3):
            icopies[k, dy].wait_recv()
        total = igf[k][y]
        for dy in (1, 2, 3):
            total = total + yr[k][dy - 1].astype(F32)
        zs[k][...] = total.astype(BF16)
        if not spreads:
            pl.semaphore_wait(relay, 2)
        spreads.append(k)
        for i, d in enumerate(CHUNKS[k]):
            for f in range(2):
                zsend(k, f, zs[k].at[f, i], d)

    def zcopy(k, f, src, d):
        slot = 2 * k + zh
        return pltpu.make_async_remote_copy(
            src_ref=src, dst_ref=zr.at[slot], send_sem=zsend_sem.at[2 * k + f], recv_sem=zrecv_sem.at[slot],
            device_id={"inp": x * 2 + (c + f) % 2, "out": c * 4 + y, "dep": (zl + d + 8) % 8},
            device_id_type=MESH,
        )

    def zsend(k, f, src, d):
        copy = zcopy(k, f, src, d)
        zcopies[k, f] = copy
        if k or f:
            copy.start()
            return

        @pl.when(zh != c)
        def _():
            copy.start()

        @pl.when(zh == c)
        def _():
            zr[zh] = src[...]

    def finish():
        for copy in sent:
            copy.wait_send()
        for k in range(len(CHUNKS)):
            for half in range(2):
                slot = zr.at[2 * k + half]
                landed = pltpu.make_async_remote_copy(
                    src_ref=slot, dst_ref=slot, send_sem=zsend_sem.at[0],
                    recv_sem=zrecv_sem.at[2 * k + half], device_id=at(dc=1), device_id_type=MESH,
                )
                if k:
                    landed.wait_recv()
                else:
                    pl.when((zh != half) | (zh != c))(landed.wait_recv)
        total = zr[0].astype(F32)
        for slot in range(1, 16):
            total = total + zr[slot].astype(F32)
        ig_buf[...] = total.astype(BF16)
        store(ig_buf, ig_out)

    def write():
        for i, result in enumerate((dg_out, gg_out, ug_out)):
            wbuf[i] = acc[i * HP : i * HP + H, :].astype(BF16)
            store(wbuf.at[i], result)

    start()
    steps = dict(
        arrive=arrive, project_x=lambda k: project(k, 0), project_g=lambda k: project(k, 1),
        join_cores=join_cores, activate=activate, share=share, backward=backward,
        weights=weights, spread=spread, write=lambda k: write(), finish=lambda k: finish(),
    )
    for name, *where in ORDER:
        steps[name](*where)
    for (k, f), copy in zcopies.items():
        if k or f:
            copy.wait_send()
        else:
            pl.when(zh != c)(copy.wait_send)
    for copy in stored:
        copy.wait()


def land(*refs):
    sources, results, held, sem_in, sem_out = refs[:4], refs[4:8], refs[8:12], refs[12], refs[13]
    loads = [pltpu.make_async_copy(sources[i], held[i], sem_in.at[i]) for i in range(4)]
    stores = [pltpu.make_async_copy(held[i], results[i], sem_out.at[i]) for i in range(4)]
    for load in loads:
        load.start()
    for load, store in zip(loads, stores):
        load.wait()
        store.start()
    for store in stores:
        store.wait()


def body(inputs, out_grad, gate_weight, up_weight, down_weight):
    any_spec = pl.BlockSpec(memory_space=pl.ANY)
    sizes = [len(c) for c in CHUNKS]

    def each(make):
        return [pltpu.VMEM(*make(n)) for n in sizes]

    wide = 3 * HP
    bufs = (
        each(lambda n: ((2, 4, n, K, wide), F32))
        + each(lambda n: ((4, n, K, wide), F32))
        + each(lambda n: ((4, n, K, wide), F32))
        + each(lambda n: ((4, n, K, wide), BF16))
        + each(lambda n: ((3, n, K, wide), BF16))
        + each(lambda n: ((2, 4, n, K, wide), BF16))
        + each(lambda n: ((4, 2, n, K, R), F32))
        + each(lambda n: ((4, 2, n, K, R), BF16))
        + each(lambda n: ((3, 2, n, K, R), BF16))
        + each(lambda n: ((2, n, K, R), BF16))
    )
    parts = pl.pallas_call(
        kernel,
        out_shape=(
            jax.ShapeDtypeStruct((K, R), BF16),
            jax.ShapeDtypeStruct((H, R), BF16),
            jax.ShapeDtypeStruct((H, R), BF16),
            jax.ShapeDtypeStruct((H, R), BF16),
        ),
        in_specs=[any_spec] * 5,
        out_specs=(any_spec,) * 4,
        scratch_shapes=[
            pltpu.VMEM((8, T, R), BF16),
            pltpu.VMEM((8, T, R), BF16),
            pltpu.VMEM((2 * HP, R), BF16),
            pltpu.VMEM((HP, R), BF16),
            pltpu.VMEM((2 * HP, R), BF16),
            pltpu.VMEM((3 * HP, R), F32),
            pltpu.VMEM((16, K, R), BF16),
            pltpu.SemaphoreType.DMA((16,)),
            pltpu.SemaphoreType.DMA((16,)),
            pltpu.VMEM((K, R), BF16),
            pltpu.VMEM((3, H, R), BF16),
            pltpu.SemaphoreType.DMA((5,)),
            pltpu.SemaphoreType.DMA((4,)),
            pltpu.SemaphoreType.DMA((N_SEM,)),
            pltpu.SemaphoreType.DMA((N_SEM,)),
            pltpu.SemaphoreType.REGULAR,
        ]
        + bufs,
        compiler_params=pltpu.CompilerParams(
            collective_id=0, has_side_effects=True, vmem_limit_bytes=56 * 2**20
        ),
        name="swiglu_backward",
    )(inputs, out_grad, gate_weight, up_weight, down_weight)
    return tuple(
        pl.pallas_call(
            land,
            out_shape=tuple(jax.ShapeDtypeStruct(p.shape, p.dtype) for p in parts),
            in_specs=[any_spec] * 4,
            out_specs=(any_spec,) * 4,
            scratch_shapes=[pltpu.VMEM(p.shape, p.dtype) for p in parts]
            + [pltpu.SemaphoreType.DMA((4,)), pltpu.SemaphoreType.DMA((4,))],
            name="land",
        )(*parts)
    )


def solution(mesh):
    return jax.shard_map(
        body,
        mesh=mesh,
        in_specs=(
            P("dep", "inp"),
            P("dep", "inp"),
            P(("out", "dep"), "inp"),
            P(("out", "dep"), "inp"),
            P(("out", "dep"), "inp"),
        ),
        out_specs=(
            P(("dep", "out"), "inp"),
            P(("out", "dep"), "inp"),
            P(("out", "dep"), "inp"),
            P(("out", "dep"), "inp"),
        ),
        check_vma=False,
    )
```
